1024 devices in a mesh: dp: 4 (over x_lo), expert: 8 (over y), tensor: 32 (over x_hi, z, core).
Axes of the slice: x: 8 (x_hi: 2, x_lo: 4; x = x_hi * 4 + x_lo), y: 8, z: 8, core: 2. Of those that a mesh axis runs over, the one named last changes fastest.
Arguments:
- tokens: bfloat16 [4096, 4096], P(('dp', 'expert'), 'tensor'), may hold values from -6 to 6
- cotangent: bfloat16 [4096, 4096], P(('dp', 'expert'), 'tensor'), may hold values from -1.1953125 to 1.1953125
- routes: int32 [4096, 2], P(('dp', 'expert')), may hold values from 0 to 7, all different within a row; in each aligned block of 128 rows (0 to 127, 128 to 255, ...) at most 64 rows name the same one
- route_weight: float32 [4096, 2], P(('dp', 'expert')), may hold values from 0.05 to 1
- w_gate_up: bfloat16 [8, 4096, 3072], P('expert', 'tensor'), may hold values from -0.09375 to 0.09375
- w_down: bfloat16 [8, 1536, 4096], P('expert', None, 'tensor'), may hold values from -0.15625 to 0.15625
Outputs:
- expert_out: bfloat16 [16384, 4096], P(('dp', 'expert'), 'tensor')
- w_down_grad: float32 [8, 1536, 4096], P('expert', 'dp', 'tensor')
The draws below stay inside these ranges and needn't reach their ends.
Inputs may be any that keep to these rules, and one draw needn't show every extreme that they name: `routes`: each row names 2 different experts. In each aligned block of 128 rows (the rows of one index pair of dp and expert) no expert is named by more than 64 rows, a bound that some block reaches.
All inputs are finite; a program needn't handle non-finite values.
Results may differ from the reference program's by a relative error of at most 0.0049.
Values may be sent and summed in bfloat16 or wider, within the bound.
No kernel may reach another device: no remote copies, remote signals or barrier semaphores. Data moves between devices by JAX's collectives and lax.ppermute only.
A program may use at most 32 MiB of HBM per device.

```python
import math
import jax
import jax.numpy as jnp
import numpy as np
from jax import lax

D = 4096
H = 1536
TOK_DEV = 128
TOP = 2
EXPERTS = 8
CAP = 64
TOKENS = 4096
N_DP = 4
N_EXPERT = 8


def steps_of(stream_key, shape, pieces, low, largest):
    level, own = 1.0, jax.random.fold_in(stream_key, 6)
    for axis_at, shards_of in pieces:
        heights = jnp.exp(jax.random.uniform(jax.random.fold_in(own, axis_at), (shards_of,), jnp.float32, low / len(pieces), largest / len(pieces)))
        level = level * jnp.repeat(heights, shape[axis_at] // shards_of).reshape([-1 if axis == axis_at else 1 for axis in range(len(shape))])
    return level


def routed_block(key, own, number, rows, number_of, top, limit, slope):
    ranking = jax.random.permutation(key, number_of)
    packed, common = portions_of(number_of, rows * top, limit, slope, True), portions_of(number_of, rows * top, limit, slope, False)
    places = jnp.arange(number_of)

    def named(sizes, rotation):
        used = int((sizes > 0).sum())
        fixed = max(1, used // 4)
        moved = fixed + (places - fixed + rotation * (used - fixed)) % max(1, number_of - fixed)
        return jnp.zeros((number_of,), jnp.int32).at[ranking[jnp.where(places < fixed, places, moved)]].set(jnp.asarray(sizes, jnp.int32))

    sizes = jnp.where(number % 4 == 0, named(packed, number // 4), named(common, number - number // 4 - 1))
    mixed = jax.random.permutation(jax.random.fold_in(own, 3), number_of)
    source_of, sink = mixed[0:number_of // 2 * 2:2], mixed[1:number_of // 2 * 2:2]
    slack = jnp.minimum(sizes[source_of] - 1, limit - sizes[sink]) // 2
    slack = jnp.where((source_of == ranking[0]) | (sink == ranking[0]) | (sizes[sink] == 0), 0, jnp.maximum(slack, 0))
    moved = jax.random.randint(jax.random.fold_in(own, 4), (number_of // 2,), 0, 1 << 20) % (slack + 1)
    sizes = sizes.at[source_of].add(-moved).at[sink].add(moved)
    members = jnp.searchsorted(jnp.cumsum(sizes), jnp.arange(rows * top), side="right").astype(jnp.int32)
    grid = members.reshape(top, rows).T
    grid = grid[jax.random.permutation(jax.random.fold_in(own, 1), rows)]
    rotation = jax.random.randint(jax.random.fold_in(own, 2), (rows, 1), 0, top)
    return jnp.take_along_axis(grid, (jnp.arange(top)[None, :] + rotation) % top, axis=1)


def portions_of(count, total, most, slope, full):
    weights = [(1 << 20) // math.isqrt(standing ** slope) + 1 for standing in range(1, count + 1)]
    largest = most if full else min(most, max(-(-total // count), total * weights[0] // sum(weights)))
    least = 1 if total - largest >= count - 1 else 0
    holding, rest = [largest] + [least] * (count - 1), total - largest - least * (count - 1)
    while rest > 0:
        movable = [i for i in range(1, count) if holding[i] < largest] or [i for i in range(1, count) if holding[i] < most]
        pool, remaining = sum([weights[i] for i in movable]), rest
        for i in movable:
            addition = min(most - holding[i], max(1, remaining * weights[i] // pool), rest)
            holding[i] = holding[i] + addition
            rest = rest - addition
    return np.array(holding)


def normal_values(stream_key, shape, width, bound, pieces=(), kind=jnp.bfloat16):
    entries = width * jax.random.normal(stream_key, shape, jnp.float32)
    if pieces:
        entries = entries * steps_of(stream_key, shape, pieces, -0.22, 0.18)
    return jnp.clip(entries, -bound, bound).astype(kind)


def setup_inputs(seed: int = 0) -> dict:
    streams_of = jax.random.split(jax.random.key(seed), 7)
    tokens = normal_values(streams_of[0], (TOKENS, D), 1.0, 6.0, ((0, 32), (1, 32)))
    cotangent = normal_values(streams_of[1], (TOKENS, D), 0.2, 1.1953125, ((0, 32), (1, 32)))
    routes_keys = jax.random.split(jax.random.fold_in(streams_of[2], 1), TOKENS // TOK_DEV)
    routes_turns = jax.random.permutation(jax.random.fold_in(streams_of[2], 3), TOKENS // TOK_DEV)
    routes = jax.vmap(lambda own, number: routed_block(jax.random.fold_in(streams_of[2], 2), own, number, TOK_DEV, EXPERTS, TOP, CAP, 2))(routes_keys, routes_turns).reshape((TOKENS, TOP))
    route_weight = jnp.clip(jnp.exp(math.log(1.0) - 2.9957323 * jax.random.uniform(streams_of[3], (TOKENS, TOP), jnp.float32) ** steps_of(streams_of[3], (TOKENS, TOP), ((0, 32),), -0.2, 0.2)), 0.05, 1.0)
    w_gate_up = normal_values(streams_of[4], (EXPERTS, D, 2 * H), D ** -0.5, 0.09375, ((0, 8), (1, 32)))
    w_down = normal_values(streams_of[5], (EXPERTS, H, D), H ** -0.5, 0.15625, ((0, 8), (2, 32)))
    return {"tokens": tokens, "cotangent": cotangent, "routes": routes, "route_weight": route_weight, "w_gate_up": w_gate_up, "w_down": w_down}


def reference(tokens, cotangent, routes, route_weight, w_gate_up, w_down):
    blocks = N_DP * N_EXPERT
    assigned = TOK_DEV * TOP
    flat_routes = routes.reshape(blocks, assigned)
    onehot = (flat_routes[:, :, None] == jnp.arange(EXPERTS, dtype=jnp.int32)[None, None, :]).astype(jnp.int32)
    before = jnp.cumsum(onehot, axis=1) - onehot
    slot_index = jnp.sum(before * onehot, axis=2)
    block_ids = jnp.arange(blocks, dtype=jnp.int32)[:, None]
    target = (((block_ids // N_EXPERT) * EXPERTS + flat_routes) * N_EXPERT + block_ids % N_EXPERT) * CAP + slot_index
    token_ids = block_ids * TOK_DEV + jnp.arange(assigned, dtype=jnp.int32)[None, :] // TOP
    target = target.reshape(-1).astype(jnp.int32)
    token_ids = token_ids.reshape(-1).astype(jnp.int32)
    rows_total = N_DP * EXPERTS * N_EXPERT * CAP
    slot_rows = jnp.zeros((rows_total, D), jnp.bfloat16).at[target].set(tokens[token_ids])
    scaled = (route_weight.reshape(-1)[:, None] * cotangent[token_ids].astype(jnp.float32)).astype(jnp.bfloat16)
    slot_grads = jnp.zeros((rows_total, D), jnp.bfloat16).at[target].set(scaled)
    owner_rows = N_EXPERT * CAP
    slot_rows = slot_rows.reshape(N_DP, EXPERTS, owner_rows, D).transpose(1, 0, 2, 3)
    slot_grads = slot_grads.reshape(N_DP, EXPERTS, owner_rows, D).transpose(1, 0, 2, 3)

    def one_expert(operands):
        rows_e, grads_e, gate_up_w, down_w = operands
        outputs = []
        grad_total = jnp.zeros((H, D), jnp.float32)
        for dp_index in range(N_DP):
            summed = jnp.dot(rows_e[dp_index], gate_up_w, preferred_element_type=jnp.float32)
            hidden = (jax.nn.silu(summed[:, :H]) * summed[:, H:]).astype(jnp.bfloat16)
            outputs.append(jnp.dot(hidden, down_w, preferred_element_type=jnp.float32).astype(jnp.bfloat16))
            grad_total = grad_total + jnp.dot(hidden.T, grads_e[dp_index], preferred_element_type=jnp.float32)
        return jnp.stack(outputs), grad_total

    results, grads = lax.map(one_expert, (slot_rows, slot_grads, w_gate_up, w_down))
    expert_out = results.transpose(1, 0, 2, 3).reshape(rows_total, D)
    return expert_out, grads
```

```python
import jax
import jax.numpy as jnp
from jax import lax
from jax.sharding import Mesh, PartitionSpec as P

BF = jnp.bfloat16
F32 = jnp.float32
XH, Z, CORE = 2, 8, 2
QUARTERS = XH * CORE


def exchange(pieces, axes):
    return lax.all_to_all(pieces, axes, split_axis=0, concat_axis=0, tiled=True)


def slots_of(routes, experts, capacity):
    tok_rows, top_count = routes.shape
    flat = routes.reshape(-1)
    onehot = (flat[:, None] == jnp.arange(experts, dtype=jnp.int32)[None, :]).astype(jnp.int32)
    before = jnp.cumsum(onehot, axis=0) - onehot
    slot = jnp.sum(before * onehot, axis=1)
    target = flat * capacity + slot
    return jnp.arange(experts * capacity, dtype=jnp.int32)[:, None] == target[None, :]


def per_device(tokens, cotangent, routes, route_weight, w_gate_up, w_down):
    tok_rows, width = tokens.shape
    experts = lax.axis_size("expert")
    dps = lax.axis_size("dp")
    top_count = routes.shape[1]
    capacity = min(tok_rows, 2 * tok_rows * top_count // experts)
    rows = experts * capacity
    hidden_units = w_gate_up.shape[2] // 2
    part = hidden_units // QUARTERS
    core = lax.axis_index("core")

    weights = w_gate_up[0].reshape(width, 2, QUARTERS, part).transpose(2, 0, 1, 3)
    weights = exchange(weights.reshape(QUARTERS, width, 2 * part), ("xh", "core"))
    weights = weights.reshape(QUARTERS * width, 2 * part)

    matches = slots_of(routes, experts, capacity)
    select = jnp.sum(
        matches.reshape(rows, tok_rows, top_count).astype(F32), axis=2
    ).astype(BF)
    sent_rows = jnp.dot(select, tokens, preferred_element_type=F32).astype(BF)
    sent_rows = sent_rows.reshape(experts, 1, capacity, width)
    sent_rows = jnp.broadcast_to(sent_rows, (experts, QUARTERS, capacity, width))
    moved = exchange(
        sent_rows.reshape(experts * QUARTERS, capacity, width), ("expert", "xh", "core")
    )
    slot_rows = moved.reshape(experts, QUARTERS, capacity, width)
    slot_rows = slot_rows.transpose(0, 2, 1, 3).reshape(rows, QUARTERS * width)

    partial = jnp.dot(slot_rows, weights, preferred_element_type=F32).astype(BF)
    moved = exchange(partial.reshape(Z, rows // Z, 2 * part), "z")

    weights_slot = jnp.sum(jnp.where(matches, route_weight.reshape(1, -1), 0.0), axis=1)
    sent_grads = (
        jnp.dot(select, cotangent, preferred_element_type=F32) * weights_slot[:, None]
    ).astype(BF)
    slot_grads = exchange(sent_grads.reshape(experts, capacity, width), "expert")
    slot_grads = slot_grads.reshape(rows, width)

    gate_up = jnp.sum(moved.astype(F32), axis=0)
    hidden = (jax.nn.silu(gate_up[:, :part]) * gate_up[:, part:]).astype(BF)

    pair = lax.all_gather(hidden, "xh", axis=0)
    spread = exchange(jnp.broadcast_to(pair[None], (Z,) + pair.shape), "z")
    mine = spread.transpose(1, 0, 2, 3).reshape(XH, rows, part)
    other = lax.ppermute(mine, "core", [(0, 1), (1, 0)])
    first = jnp.where(core == 0, mine, other)
    second = jnp.where(core == 0, other, mine)
    whole = jnp.stack([first, second], axis=1).reshape(QUARTERS, rows, part)

    down = w_down[0].reshape(QUARTERS, part, width)
    grads = lax.dot_general(
        whole, slot_grads, (((1,), (0,)), ((), ())), preferred_element_type=F32
    ).astype(BF)
    moved = exchange(grads.reshape(dps, hidden_units // dps, width), "dp")
    outputs = lax.dot_general(
        whole, down, (((0, 2), (0, 1)), ((), ())), preferred_element_type=F32
    ).astype(BF)
    grad_share = jnp.sum(moved.astype(F32), axis=0)
    return outputs, grad_share[None]


def solution(mesh):
    dps, experts = mesh.shape["dp"], mesh.shape["expert"]
    fine = Mesh(
        mesh.devices.reshape(dps, experts, XH, Z, CORE), ("dp", "expert", "xh", "z", "core")
    )
    tensor = ("xh", "z", "core")
    in_specs = (
        P(("dp", "expert"), tensor),
        P(("dp", "expert"), tensor),
        P(("dp", "expert"), None),
        P(("dp", "expert"), None),
        P("expert", tensor, None),
        P("expert", None, tensor),
    )
    out_specs = (P(("dp", "expert"), tensor), P("expert", "dp", tensor))
    return jax.shard_map(
        per_device, mesh=fine, in_specs=in_specs, out_specs=out_specs, check_vma=False
    )
```

```python
import jax
import jax.numpy as jnp
from jax import lax
from jax.sharding import Mesh, PartitionSpec as P

BF = jnp.bfloat16
F32 = jnp.float32
XH, Z, CORE = 2, 8, 2
QUARTERS = XH * CORE
SWAP = [(0, 1), (1, 0)]


def exchange(pieces, axes):
    return lax.all_to_all(pieces, axes, split_axis=0, concat_axis=0, tiled=True)


def dot(a, b):
    return jnp.dot(a, b, preferred_element_type=F32)


def pick(index, pair):
    first = index == 0
    return jnp.where(first, pair[0], pair[1]), jnp.where(first, pair[1], pair[0])


def slots_of(routes, experts, capacity):
    flat = routes.reshape(-1)
    onehot = (flat[:, None] == jnp.arange(experts, dtype=jnp.int32)[None, :]).astype(jnp.int32)
    before = jnp.cumsum(onehot, axis=0) - onehot
    slot = jnp.sum(before * onehot, axis=1)
    target = flat * capacity + slot
    return jnp.arange(experts * capacity, dtype=jnp.int32)[:, None] == target[None, :]


def per_device(tokens, cotangent, routes, route_weight, w_gate_up, w_down):
    tok_rows, width = tokens.shape
    experts = lax.axis_size("expert")
    dps = lax.axis_size("dp")
    top_count = routes.shape[1]
    capacity = min(tok_rows, 2 * tok_rows * top_count // experts)
    rows = experts * capacity
    hidden_units = w_gate_up.shape[2] // 2
    part = hidden_units // QUARTERS
    core = lax.axis_index("core")
    xh = lax.axis_index("xh")

    far_tokens = lax.ppermute(tokens, "xh", SWAP)

    blocks = w_gate_up[0].reshape(width, 2, XH, CORE, part).transpose(3, 2, 0, 1, 4)
    blocks = blocks.reshape(CORE, XH, width, 2 * part)
    own, theirs = pick(core, blocks)
    beside = lax.ppermute(theirs, "core", SWAP)
    near = jnp.stack([own, beside], axis=1)
    near_own, near_theirs = pick(xh, near)
    far = lax.ppermute(near_theirs, "xh", SWAP)
    w_mine = jnp.concatenate([near_own[0], far[0]], axis=0)
    w_beside = jnp.concatenate([near_own[1], far[1]], axis=0)

    matches = slots_of(routes, experts, capacity)
    select = jnp.sum(
        matches.reshape(rows, tok_rows, top_count).astype(F32), axis=2
    ).astype(BF)
    weights_slot = jnp.sum(jnp.where(matches, route_weight.reshape(1, -1), 0.0), axis=1)
    sent_grads = (dot(select, cotangent) * weights_slot[:, None]).astype(BF)
    sent_rows = dot(select, jnp.concatenate([tokens, far_tokens], axis=1)).astype(BF)
    sent = jnp.concatenate([sent_rows, sent_grads], axis=1)
    moved = exchange(sent.reshape(experts, capacity, 3 * width), "expert")
    moved = moved.reshape(rows, 3 * width)
    mine, slot_grads = moved[:, : 2 * width], moved[:, 2 * width :]
    beside_rows = lax.ppermute(mine, "core", SWAP)

    partial = (dot(mine, w_mine) + dot(beside_rows, w_beside)).astype(BF)
    moved = exchange(partial.reshape(Z, rows // Z, 2 * part), "z")
    gate_up = jnp.sum(moved.astype(F32), axis=0)
    hidden = (jax.nn.silu(gate_up[:, :part]) * gate_up[:, part:]).astype(BF)

    spread = exchange(jnp.broadcast_to(hidden[None], (XH * Z,) + hidden.shape), ("xh", "z"))
    hid_mine = spread.reshape(XH, rows, part)
    hid_beside = lax.ppermute(hid_mine, "core", SWAP)

    def grads_of(hid):
        return lax.dot_general(
            hid, slot_grads, (((1,), (0,)), ((), ())), preferred_element_type=F32
        ).astype(BF)

    def outs_of(hid, down):
        return lax.dot_general(
            hid, down, (((0, 2), (0, 1)), ((), ())), preferred_element_type=F32
        )

    grads = jnp.stack([grads_of(hid_mine), grads_of(hid_beside)])
    grads = jnp.stack(pick(core, grads), axis=1)
    moved = exchange(grads.reshape(dps, hidden_units // dps, width), "dp")
    down = w_down[0].reshape(XH, CORE, part, width).transpose(1, 0, 2, 3)
    down_mine, down_beside = pick(core, down)
    outputs = (outs_of(hid_mine, down_mine) + outs_of(hid_beside, down_beside)).astype(BF)
    grad_share = jnp.sum(moved.astype(F32), axis=0)
    return outputs, grad_share[None]


def solution(mesh):
    dps, experts = mesh.shape["dp"], mesh.shape["expert"]
    fine = Mesh(
        mesh.devices.reshape(dps, experts, XH, Z, CORE), ("dp", "expert", "xh", "z", "core")
    )
    tensor = ("xh", "z", "core")
    in_specs = (
        P(("dp", "expert"), tensor),
        P(("dp", "expert"), tensor),
        P(("dp", "expert"), None),
        P(("dp", "expert"), None),
        P("expert", tensor, None),
        P("expert", None, tensor),
    )
    out_specs = (P(("dp", "expert"), tensor), P("expert", "dp", tensor))
    return jax.shard_map(
        per_device, mesh=fine, in_specs=in_specs, out_specs=out_specs, check_vma=False
    )
```

```python
import jax
import jax.numpy as jnp
from jax import lax
from jax.sharding import Mesh, PartitionSpec as P

BF = jnp.bfloat16
F32 = jnp.float32
XH, ZH, ZL, CORE = 2, 4, 2, 2
QUARTERS = ZL * CORE
ROWS_AXES = ("xh", "zh")
SWAP = [(0, 1), (1, 0)]


def exchange(pieces, axes):
    return lax.all_to_all(pieces, axes, split_axis=0, concat_axis=0, tiled=True)


def dot(a, b):
    return jnp.dot(a, b, preferred_element_type=F32)


def pick(index, pair):
    first = index == 0
    return jnp.where(first, pair[0], pair[1]), jnp.where(first, pair[1], pair[0])


def slots_of(routes, experts, capacity):
    flat = routes.reshape(-1)
    onehot = (flat[:, None] == jnp.arange(experts, dtype=jnp.int32)[None, :]).astype(jnp.int32)
    before = jnp.cumsum(onehot, axis=0) - onehot
    slot = jnp.sum(before * onehot, axis=1)
    target = flat * capacity + slot
    return jnp.arange(experts * capacity, dtype=jnp.int32)[:, None] == target[None, :]


def per_device(tokens, cotangent, routes, route_weight, w_gate_up, w_down):
    tok_rows, width = tokens.shape
    experts = lax.axis_size("expert")
    dps = lax.axis_size("dp")
    top_count = routes.shape[1]
    capacity = min(tok_rows, 2 * tok_rows * top_count // experts)
    rows = experts * capacity
    hidden_units = w_gate_up.shape[2] // 2
    part = hidden_units // QUARTERS
    core = lax.axis_index("core")
    zl = lax.axis_index("zl")

    far_tokens = lax.ppermute(tokens, "zl", SWAP)

    blocks = w_gate_up[0].reshape(width, 2, ZL, CORE, part).transpose(2, 3, 0, 1, 4)
    blocks = blocks.reshape(ZL, CORE, width, 2 * part)
    own, theirs = pick(zl, blocks)
    far = lax.ppermute(theirs, "zl", SWAP)
    own_mine, own_theirs = pick(core, own)
    far_mine, far_theirs = pick(core, far)
    w_mine = jnp.concatenate([own_mine, far_mine], axis=0)
    w_beside = lax.ppermute(jnp.concatenate([own_theirs, far_theirs], axis=0), "core", SWAP)

    matches = slots_of(routes, experts, capacity)
    select = jnp.sum(
        matches.reshape(rows, tok_rows, top_count).astype(F32), axis=2
    ).astype(BF)
    weights_slot = jnp.sum(jnp.where(matches, route_weight.reshape(1, -1), 0.0), axis=1)
    sent = dot(select, jnp.concatenate([tokens, far_tokens, cotangent], axis=1))
    is_token = jnp.arange(3 * width, dtype=jnp.int32)[None, :] < 2 * width
    sent = (sent * jnp.where(is_token, 1.0, weights_slot[:, None])).astype(BF)
    moved = exchange(sent.reshape(experts, capacity, 3 * width), "expert")
    moved = moved.reshape(rows, 3 * width)
    mine, slot_grads = moved[:, : 2 * width], moved[:, 2 * width :]
    beside_rows = lax.ppermute(mine, "core", SWAP)

    partial = (dot(mine, w_mine) + dot(beside_rows, w_beside)).astype(BF)
    groups = XH * ZH
    moved = exchange(partial.reshape(groups, rows // groups, 2 * part), ROWS_AXES)
    gate_up = jnp.sum(moved.astype(F32), axis=0)
    hidden = (jax.nn.silu(gate_up[:, :part]) * gate_up[:, part:]).astype(BF)

    spread = exchange(
        jnp.broadcast_to(hidden[None], (groups * ZL,) + hidden.shape), ROWS_AXES + ("zl",)
    )
    spread = spread.reshape(groups, ZL, rows // groups, part).transpose(1, 0, 2, 3)
    hid_mine = spread.reshape(ZL, rows, part)
    hid_beside = lax.ppermute(hid_mine, "core", SWAP)

    def grads_of(hid):
        return lax.dot_general(
            hid, slot_grads, (((1,), (0,)), ((), ())), preferred_element_type=F32
        ).astype(BF)

    def outs_of(hid, down):
        return lax.dot_general(
            hid, down, (((0, 2), (0, 1)), ((), ())), preferred_element_type=F32
        )

    grads = jnp.stack([grads_of(hid_mine), grads_of(hid_beside)])
    grads = jnp.stack(pick(core, grads), axis=1)
    moved = exchange(grads.reshape(dps, hidden_units // dps, width), "dp")
    down = w_down[0].reshape(ZL, CORE, part, width).transpose(1, 0, 2, 3)
    down_mine, down_beside = pick(core, down)
    outputs = (outs_of(hid_mine, down_mine) + outs_of(hid_beside, down_beside)).astype(BF)
    grad_share = jnp.sum(moved.astype(F32), axis=0)
    return outputs, grad_share[None]


def solution(mesh):
    dps, experts = mesh.shape["dp"], mesh.shape["expert"]
    fine = Mesh(
        mesh.devices.reshape(dps, experts, XH, ZH, ZL, CORE),
        ("dp", "expert", "xh", "zh", "zl", "core"),
    )
    tensor = ("xh", "zh", "zl", "core")
    in_specs = (
        P(("dp", "expert"), tensor),
        P(("dp", "expert"), tensor),
        P(("dp", "expert"), None),
        P(("dp", "expert"), None),
        P("expert", tensor, None),
        P("expert", None, tensor),
    )
    out_specs = (P(("dp", "expert"), tensor), P("expert", "dp", tensor))
    return jax.shard_map(
        per_device, mesh=fine, in_specs=in_specs, out_specs=out_specs, check_vma=False
    )
```

```python
import jax
import jax.numpy as jnp
from jax import lax
from jax.sharding import Mesh, PartitionSpec as P

BF = jnp.bfloat16
F32 = jnp.float32
XH, Z, CORE = 2, 8, 2
QUARTERS = XH * CORE
SWAP = [(0, 1), (1, 0)]


def exchange(pieces, axes):
    return lax.all_to_all(pieces, axes, split_axis=0, concat_axis=0, tiled=True)


def dot(a, b):
    return jnp.dot(a, b, preferred_element_type=F32)


def pick(index, pair):
    first = index == 0
    return jnp.where(first, pair[0], pair[1]), jnp.where(first, pair[1], pair[0])


def slots_of(routes, experts, capacity):
    flat = routes.reshape(-1)
    onehot = (flat[:, None] == jnp.arange(experts, dtype=jnp.int32)[None, :]).astype(jnp.int32)
    before = jnp.cumsum(onehot, axis=0) - onehot
    slot = jnp.sum(before * onehot, axis=1)
    target = flat * capacity + slot
    return jnp.arange(experts * capacity, dtype=jnp.int32)[:, None] == target[None, :]


def after(index, array):
    return index + jnp.minimum(jnp.abs(array[0, 0]).astype(jnp.int32), 0)


def to_quarters(blocks, xh, core):
    near, sent = pick(xh, blocks)
    far = lax.ppermute(sent, "xh", SWAP)
    near_mine, near_sent = pick(core, near)
    far_mine, far_sent = pick(core, far)
    mine = jnp.stack([near_mine, far_mine])
    beside = lax.ppermute(jnp.stack([near_sent, far_sent]), "core", SWAP)
    return mine, beside


def per_device(tokens, cotangent, routes, route_weight, w_gate_up, w_down):
    tok_rows, width = tokens.shape
    experts = lax.axis_size("expert")
    dps = lax.axis_size("dp")
    top_count = routes.shape[1]
    capacity = min(tok_rows, 2 * tok_rows * top_count // experts)
    rows = experts * capacity
    hidden_units = w_gate_up.shape[2] // 2
    part = hidden_units // QUARTERS
    step = part // dps
    core = lax.axis_index("core")
    xh = lax.axis_index("xh")

    far_tokens = lax.ppermute(tokens, "xh", SWAP)

    matches = slots_of(routes, experts, capacity)
    select = jnp.sum(
        matches.reshape(rows, tok_rows, top_count).astype(F32), axis=2
    ).astype(BF)
    w = w_gate_up[0].reshape(width, 2, dps, XH, CORE, step).transpose(3, 4, 0, 1, 2, 5)
    w_mine, w_beside = to_quarters(
        w.reshape(XH, CORE, width, 2 * part), after(xh, far_tokens), core
    )

    weights_slot = jnp.sum(jnp.where(matches, route_weight.reshape(1, -1), 0.0), axis=1)
    sent = dot(select, jnp.concatenate([tokens, far_tokens, cotangent], axis=1))
    is_token = jnp.arange(3 * width, dtype=jnp.int32)[None, :] < 2 * width
    sent = (sent * jnp.where(is_token, 1.0, weights_slot[:, None])).astype(BF)
    mine = exchange(sent.reshape(experts, capacity, 3 * width), "expert")
    mine = mine.reshape(rows, 3 * width)
    beside = lax.ppermute(mine, "core", SWAP)

    partial = dot(mine[:, : 2 * width], w_mine.reshape(2 * width, 2 * part))
    partial += dot(beside[:, : 2 * width], w_beside.reshape(2 * width, 2 * part))
    moved = exchange(partial.astype(BF).reshape(Z, rows // Z, 2 * part), "z")
    gate_up = jnp.sum(moved.astype(F32), axis=0)
    hidden = (jax.nn.silu(gate_up[:, :part]) * gate_up[:, part:]).astype(BF)
    hidden = exchange(jnp.broadcast_to(hidden[None], (Z,) + hidden.shape), "z")
    hidden = hidden.reshape(rows, part)

    near_grads = jnp.stack([mine[:, 2 * width :], beside[:, 2 * width :]])
    far_grads = lax.ppermute(near_grads, "xh", SWAP)
    by_xh = pick(after(xh, gate_up), jnp.stack([near_grads, far_grads]))
    slot_grads = [g for pair in by_xh for g in pick(core, pair)]
    grads = [
        lax.dot_general(
            hidden, g, (((0,), (0,)), ((), ())), preferred_element_type=F32
        ).astype(BF)
        for g in slot_grads
    ]
    grads = jnp.stack([g.reshape(dps, step, width) for g in grads], axis=1)
    moved = exchange(grads.reshape(dps * QUARTERS, step, width), ("dp", "xh", "core"))
    moved = moved.reshape(dps, QUARTERS * step, width)
    grad_share = jnp.sum(moved.astype(F32), axis=0)

    down = w_down[0].reshape(dps, XH, CORE, step, width).transpose(1, 2, 0, 3, 4)
    down_mine, down_beside = to_quarters(
        down.reshape(XH, CORE, part, width), after(xh, mine), after(core, gate_up)
    )
    terms = [dot(hidden, d) for d in (down_beside[0], down_beside[1])]
    came = lax.ppermute(jnp.stack(terms), "core", SWAP)
    far_sum = dot(hidden, down_mine[1]) + came[1]
    near_sum = dot(hidden, down_mine[0]) + came[0]
    outputs = near_sum + lax.ppermute(far_sum.astype(BF), "xh", SWAP).astype(F32)
    return outputs.astype(BF), grad_share[None]


def solution(mesh):
    dps, experts = mesh.shape["dp"], mesh.shape["expert"]
    fine = Mesh(
        mesh.devices.reshape(dps, experts, XH, Z, CORE), ("dp", "expert", "xh", "z", "core")
    )
    tensor = ("xh", "z", "core")
    in_specs = (
        P(("dp", "expert"), tensor),
        P(("dp", "expert"), tensor),
        P(("dp", "expert"), None),
        P(("dp", "expert"), None),
        P("expert", tensor, None),
        P("expert", None, tensor),
    )
    out_specs = (P(("dp", "expert"), tensor), P("expert", "dp", tensor))
    return jax.shard_map(
        per_device, mesh=fine, in_specs=in_specs, out_specs=out_specs, check_vma=False
    )
```

```python
import jax
import jax.numpy as jnp
from jax import lax
from jax.sharding import Mesh, PartitionSpec as P

BF = jnp.bfloat16
F32 = jnp.float32
XH, Z, CORE = 2, 8, 2
QUARTERS = XH * CORE
SWAP = [(0, 1), (1, 0)]


def exchange(pieces, axes):
    return lax.all_to_all(pieces, axes, split_axis=0, concat_axis=0, tiled=True)


def dot(a, b):
    return jnp.dot(a, b, preferred_element_type=F32)


def pick(index, pair):
    first = index == 0
    return jnp.where(first, pair[0], pair[1]), jnp.where(first, pair[1], pair[0])


def slots_of(routes, experts, capacity):
    flat = routes.reshape(-1)
    onehot = (flat[:, None] == jnp.arange(experts, dtype=jnp.int32)[None, :]).astype(jnp.int32)
    before = jnp.cumsum(onehot, axis=0) - onehot
    slot = jnp.sum(before * onehot, axis=1)
    target = flat * capacity + slot
    return jnp.arange(experts * capacity, dtype=jnp.int32)[:, None] == target[None, :]


def to_quarters(blocks, xh, core):
    near, sent = pick(xh, blocks)
    far = lax.ppermute(sent, "xh", SWAP)
    near_mine, near_sent = pick(core, near)
    far_mine, far_sent = pick(core, far)
    mine = jnp.stack([near_mine, far_mine])
    beside = lax.ppermute(jnp.stack([near_sent, far_sent]), "core", SWAP)
    return mine, beside


def per_device(tokens, cotangent, routes, route_weight, w_gate_up, w_down):
    tok_rows, width = tokens.shape
    experts = lax.axis_size("expert")
    dps = lax.axis_size("dp")
    top_count = routes.shape[1]
    capacity = min(tok_rows, 2 * tok_rows * top_count // experts)
    rows = experts * capacity
    hidden_units = w_gate_up.shape[2] // 2
    part = hidden_units // QUARTERS
    step = part // dps
    core = lax.axis_index("core")
    xh = lax.axis_index("xh")

    far_tokens = lax.ppermute(tokens, "xh", SWAP)

    matches = slots_of(routes, experts, capacity)
    select = jnp.sum(
        matches.reshape(rows, tok_rows, top_count).astype(F32), axis=2
    ).astype(BF)
    w = w_gate_up[0].reshape(width, 2, dps, XH, CORE, step).transpose(3, 4, 0, 1, 2, 5)
    w_mine, w_beside = to_quarters(
        w.reshape(XH, CORE, width, 2 * part), xh, core
    )

    weights_slot = jnp.sum(jnp.where(matches, route_weight.reshape(1, -1), 0.0), axis=1)
    sent = dot(select, jnp.concatenate([tokens, far_tokens, cotangent], axis=1))
    is_token = jnp.arange(3 * width, dtype=jnp.int32)[None, :] < 2 * width
    sent = (sent * jnp.where(is_token, 1.0, weights_slot[:, None])).astype(BF)
    mine = exchange(sent.reshape(experts, capacity, 3 * width), "expert")
    mine = mine.reshape(rows, 3 * width)
    beside = lax.ppermute(mine, "core", SWAP)

    partial = dot(mine[:, : 2 * width], w_mine.reshape(2 * width, 2 * part))
    partial += dot(beside[:, : 2 * width], w_beside.reshape(2 * width, 2 * part))
    moved = exchange(partial.astype(BF).reshape(Z, rows // Z, 2 * part), "z")
    gate_up = jnp.sum(moved.astype(F32), axis=0)
    hidden = (jax.nn.silu(gate_up[:, :part]) * gate_up[:, part:]).astype(BF)
    hidden = exchange(jnp.broadcast_to(hidden[None], (XH * Z,) + hidden.shape), ("xh", "z"))
    hidden = hidden.reshape(XH, rows, part)

    slot_grads = pick(core, jnp.stack([mine[:, 2 * width :], beside[:, 2 * width :]]))

    def grads_of(half, g):
        out = lax.dot_general(half, g, (((0,), (0,)), ((), ())), preferred_element_type=F32)
        return out.astype(BF).reshape(dps, step, width)

    grads = jnp.stack(
        [jnp.stack([grads_of(hidden[h], g) for h in range(XH)], axis=1) for g in slot_grads],
        axis=1,
    )
    moved = exchange(grads.reshape(dps * CORE, XH * step, width), ("dp", "core"))
    moved = jnp.sum(moved.reshape(dps, CORE, XH, step, width).astype(F32), axis=0)
    grad_share = moved.transpose(1, 0, 2, 3).reshape(QUARTERS * step, width)

    down = w_down[0].reshape(dps, XH, CORE, step, width).transpose(2, 1, 0, 3, 4)
    down_mine, down_sent = pick(core, down.reshape(CORE, XH, part, width))
    down_beside = lax.ppermute(down_sent, "core", SWAP)

    def terms(down):
        return dot(hidden[0], down[0]) + dot(hidden[1], down[1])

    outputs = terms(down_mine) + lax.ppermute(terms(down_beside), "core", SWAP)
    return outputs.astype(BF), grad_share[None]


def solution(mesh):
    dps, experts = mesh.shape["dp"], mesh.shape["expert"]
    fine = Mesh(
        mesh.devices.reshape(dps, experts, XH, Z, CORE), ("dp", "expert", "xh", "z", "core")
    )
    tensor = ("xh", "z", "core")
    in_specs = (
        P(("dp", "expert"), tensor),
        P(("dp", "expert"), tensor),
        P(("dp", "expert"), None),
        P(("dp", "expert"), None),
        P("expert", tensor, None),
        P("expert", None, tensor),
    )
    out_specs = (P(("dp", "expert"), tensor), P("expert", "dp", tensor))
    return jax.shard_map(
        per_device, mesh=fine, in_specs=in_specs, out_specs=out_specs, check_vma=False
    )
```

```python
import jax
import jax.numpy as jnp
from jax import lax
from jax.sharding import Mesh, PartitionSpec as P

BF = jnp.bfloat16
F32 = jnp.float32
XH, ZH, ZL, CORE = 2, 4, 2, 2
QUARTERS = ZL * CORE
SPREAD = ("xh", "zh")
SWAP = [(0, 1), (1, 0)]


def exchange(pieces, axes):
    return lax.all_to_all(pieces, axes, split_axis=0, concat_axis=0, tiled=True)


def dot(a, b):
    return jnp.dot(a, b, preferred_element_type=F32)


def pick(index, pair):
    first = index == 0
    return jnp.where(first, pair[0], pair[1]), jnp.where(first, pair[1], pair[0])


def slots_of(routes, experts, capacity):
    flat = routes.reshape(-1)
    onehot = (flat[:, None] == jnp.arange(experts, dtype=jnp.int32)[None, :]).astype(jnp.int32)
    before = jnp.cumsum(onehot, axis=0) - onehot
    slot = jnp.sum(before * onehot, axis=1)
    target = flat * capacity + slot
    return jnp.arange(experts * capacity, dtype=jnp.int32)[:, None] == target[None, :]


def after(array, earlier):
    return lax.optimization_barrier((array, earlier))[0]


def to_quarters(blocks, zl, core, earlier):
    near, sent = pick(zl, blocks)
    far = after(lax.ppermute(sent, "zl", SWAP), earlier)
    near_mine, near_sent = pick(core, near)
    far_mine, far_sent = pick(core, far)
    mine = jnp.stack([near_mine, far_mine])
    beside = lax.ppermute(jnp.stack([near_sent, far_sent]), "core", SWAP)
    return mine, beside


def per_device(tokens, cotangent, routes, route_weight, w_gate_up, w_down):
    tok_rows, width = tokens.shape
    experts = lax.axis_size("expert")
    dps = lax.axis_size("dp")
    top_count = routes.shape[1]
    capacity = min(tok_rows, 2 * tok_rows * top_count // experts)
    rows = experts * capacity
    hidden_units = w_gate_up.shape[2] // 2
    part = hidden_units // QUARTERS
    step = part // dps
    core = lax.axis_index("core")
    zl = lax.axis_index("zl")

    far_tokens = lax.ppermute(tokens, "zl", SWAP)
    far_cotangent = lax.ppermute(cotangent, "zl", SWAP)
    tokens, cotangent, w_gate_up = lax.optimization_barrier((tokens, cotangent, w_gate_up))

    matches = slots_of(routes, experts, capacity)
    select = jnp.sum(
        matches.reshape(rows, tok_rows, top_count).astype(F32), axis=2
    ).astype(BF)
    w = w_gate_up[0].reshape(width, 2, dps, ZL, CORE, step).transpose(3, 4, 0, 1, 2, 5)
    w_mine, w_beside = to_quarters(w.reshape(ZL, CORE, width, 2 * part), zl, core, ())

    weights_slot = jnp.sum(jnp.where(matches, route_weight.reshape(1, -1), 0.0), axis=1)
    sent = dot(
        select, jnp.concatenate([tokens, far_tokens, cotangent, far_cotangent], axis=1)
    )
    is_token = jnp.arange(4 * width, dtype=jnp.int32)[None, :] < 2 * width
    sent = (sent * jnp.where(is_token, 1.0, weights_slot[:, None])).astype(BF)
    mine = exchange(sent.reshape(experts, capacity, 4 * width), "expert")
    mine = mine.reshape(rows, 4 * width)
    beside = lax.ppermute(mine, "core", SWAP)

    partial = dot(mine[:, : 2 * width], w_mine.reshape(2 * width, 2 * part))
    partial += dot(beside[:, : 2 * width], w_beside.reshape(2 * width, 2 * part))
    groups = XH * ZH
    moved = exchange(partial.astype(BF).reshape(groups, rows // groups, 2 * part), SPREAD)
    gate_up = jnp.sum(moved.astype(F32), axis=0)
    hidden = (jax.nn.silu(gate_up[:, :part]) * gate_up[:, part:]).astype(BF)
    hidden = exchange(jnp.broadcast_to(hidden[None], (groups,) + hidden.shape), SPREAD)
    hidden = hidden.reshape(rows, part)

    by_core = pick(core, jnp.stack([mine[:, 2 * width :], beside[:, 2 * width :]]))
    by_core = [pick(zl, jnp.stack([g[:, :width], g[:, width:]])) for g in by_core]
    slot_grads = [by_core[c][h] for h in range(ZL) for c in range(CORE)]
    slot_grads = jnp.concatenate(slot_grads, axis=1)

    down = w_down[0].reshape(dps, ZL, CORE, step, width).transpose(1, 2, 0, 3, 4)
    down = after(down.reshape(ZL, CORE, part, width), sent)
    down_mine, down_beside = to_quarters(down, zl, core, mine)
    terms = dot(hidden, jnp.concatenate([down_beside[0], down_beside[1]], axis=1))
    came = lax.ppermute(terms, "core", SWAP)
    terms = dot(hidden, jnp.concatenate([down_mine[0], down_mine[1]], axis=1)) + came
    far_terms = terms[:, width:].astype(BF)
    outputs = terms[:, :width] + lax.ppermute(far_terms, "zl", SWAP).astype(F32)

    grads = lax.dot_general(
        hidden, slot_grads, (((0,), (0,)), ((), ())), preferred_element_type=F32
    ).astype(BF)
    grads = jnp.stack(
        [g.reshape(dps, step, width) for g in jnp.split(grads, QUARTERS, axis=1)], axis=1
    )
    moved = exchange(grads.reshape(dps * QUARTERS, step, width), ("dp", "zl", "core"))
    moved = moved.reshape(dps, QUARTERS * step, width)
    grad_share = jnp.sum(moved.astype(F32), axis=0)
    return outputs.astype(BF), grad_share[None]


def solution(mesh):
    dps, experts = mesh.shape["dp"], mesh.shape["expert"]
    fine = Mesh(
        mesh.devices.reshape(dps, experts, XH, ZH, ZL, CORE),
        ("dp", "expert", "xh", "zh", "zl", "core"),
    )
    tensor = ("xh", "zh", "zl", "core")
    in_specs = (
        P(("dp", "expert"), tensor),
        P(("dp", "expert"), tensor),
        P(("dp", "expert"), None),
        P(("dp", "expert"), None),
        P("expert", tensor, None),
        P("expert", None, tensor),
    )
    out_specs = (P(("dp", "expert"), tensor), P("expert", "dp", tensor))
    return jax.shard_map(
        per_device, mesh=fine, in_specs=in_specs, out_specs=out_specs, check_vma=False
    )
```

```python
import jax
import jax.numpy as jnp
from jax import lax
from jax.sharding import Mesh, PartitionSpec as P

BF = jnp.bfloat16
F32 = jnp.float32
XH, Z, CORE = 2, 8, 2
QUARTERS = XH * CORE
SWAP = [(0, 1), (1, 0)]


def exchange(pieces, axes):
    return lax.all_to_all(pieces, axes, split_axis=0, concat_axis=0, tiled=True)


def dot(a, b):
    return jnp.dot(a, b, preferred_element_type=F32)


def pick(index, pair):
    first = index == 0
    return jnp.where(first, pair[0], pair[1]), jnp.where(first, pair[1], pair[0])


def slots_of(routes, experts, capacity):
    flat = routes.reshape(-1)
    onehot = (flat[:, None] == jnp.arange(experts, dtype=jnp.int32)[None, :]).astype(jnp.int32)
    before = jnp.cumsum(onehot, axis=0) - onehot
    slot = jnp.sum(before * onehot, axis=1)
    target = flat * capacity + slot
    return jnp.arange(experts * capacity, dtype=jnp.int32)[:, None] == target[None, :]


def after(array, earlier):
    return lax.optimization_barrier((array, earlier))[0]


def to_quarters(blocks, xh, core, earlier=()):
    near, sent = pick(xh, blocks)
    far = after(lax.ppermute(sent, "xh", SWAP), earlier)
    near_mine, near_sent = pick(core, near)
    far_mine, far_sent = pick(core, far)
    mine = jnp.stack([near_mine, far_mine])
    beside = lax.ppermute(jnp.stack([near_sent, far_sent]), "core", SWAP)
    return mine, beside


def per_device(tokens, cotangent, routes, route_weight, w_gate_up, w_down):
    tok_rows, width = tokens.shape
    experts = lax.axis_size("expert")
    dps = lax.axis_size("dp")
    top_count = routes.shape[1]
    capacity = min(tok_rows, 2 * tok_rows * top_count // experts)
    rows = experts * capacity
    hidden_units = w_gate_up.shape[2] // 2
    part = hidden_units // QUARTERS
    step = part // dps
    core = lax.axis_index("core")
    xh = lax.axis_index("xh")

    far_tokens = lax.ppermute(tokens, "xh", SWAP)
    tokens, cotangent, w_gate_up = lax.optimization_barrier((tokens, cotangent, w_gate_up))

    matches = slots_of(routes, experts, capacity)
    select = jnp.sum(
        matches.reshape(rows, tok_rows, top_count).astype(F32), axis=2
    ).astype(BF)
    w = w_gate_up[0].reshape(width, 2, dps, XH, CORE, step).transpose(3, 4, 0, 1, 2, 5)
    w_mine, w_beside = to_quarters(
        w.reshape(XH, CORE, width, 2 * part), xh, core
    )

    weights_slot = jnp.sum(jnp.where(matches, route_weight.reshape(1, -1), 0.0), axis=1)
    sent = dot(select, jnp.concatenate([tokens, far_tokens, cotangent], axis=1))
    is_token = jnp.arange(3 * width, dtype=jnp.int32)[None, :] < 2 * width
    sent = (sent * jnp.where(is_token, 1.0, weights_slot[:, None])).astype(BF)
    mine = exchange(sent.reshape(experts, capacity, 3 * width), "expert")
    mine = mine.reshape(rows, 3 * width)
    beside = lax.ppermute(mine, "core", SWAP)

    partial = dot(mine[:, : 2 * width], w_mine.reshape(2 * width, 2 * part))
    partial += dot(beside[:, : 2 * width], w_beside.reshape(2 * width, 2 * part))
    moved = exchange(partial.astype(BF).reshape(Z, rows // Z, 2 * part), "z")
    gate_up = jnp.sum(moved.astype(F32), axis=0)
    hidden = (jax.nn.silu(gate_up[:, :part]) * gate_up[:, part:]).astype(BF)
    hidden = exchange(jnp.broadcast_to(hidden[None], (Z,) + hidden.shape), "z")
    hidden = hidden.reshape(rows, part)

    down = w_down[0].reshape(dps, XH, CORE, step, width).transpose(2, 1, 0, 3, 4)
    down_near, down_sent = pick(core, after(down.reshape(CORE, XH, part, width), sent))
    down_near = jnp.stack([down_near, lax.ppermute(down_sent, "core", SWAP)], axis=1)
    down_near, down_sent = pick(xh, after(down_near, mine))
    down_far = lax.ppermute(down_sent, "xh", SWAP)

    near_grads = jnp.stack([mine[:, 2 * width :], beside[:, 2 * width :]])
    far_grads = after(lax.ppermute(near_grads, "xh", SWAP), down_far)
    by_xh = pick(xh, jnp.stack([near_grads, far_grads]))
    slot_grads = jnp.concatenate([g for pair in by_xh for g in pick(core, pair)], axis=1)

    terms = dot(hidden, jnp.concatenate([down_near[1], down_far[1]], axis=1))
    came = lax.ppermute(terms, "core", SWAP)
    terms = dot(hidden, jnp.concatenate([down_near[0], down_far[0]], axis=1)) + came
    far_terms = terms[:, width:].astype(BF)
    outputs = terms[:, :width] + lax.ppermute(far_terms, "xh", SWAP).astype(F32)

    grads = lax.dot_general(
        hidden, slot_grads, (((0,), (0,)), ((), ())), preferred_element_type=F32
    ).astype(BF)
    grads = jnp.stack(
        [g.reshape(dps, step, width) for g in jnp.split(grads, QUARTERS, axis=1)], axis=1
    )
    moved = exchange(grads.reshape(dps * QUARTERS, step, width), ("dp", "xh", "core"))
    moved = moved.reshape(dps, QUARTERS * step, width)
    grad_share = jnp.sum(moved.astype(F32), axis=0)
    return outputs.astype(BF), grad_share[None]


def solution(mesh):
    dps, experts = mesh.shape["dp"], mesh.shape["expert"]
    fine = Mesh(
        mesh.devices.reshape(dps, experts, XH, Z, CORE), ("dp", "expert", "xh", "z", "core")
    )
    tensor = ("xh", "z", "core")
    in_specs = (
        P(("dp", "expert"), tensor),
        P(("dp", "expert"), tensor),
        P(("dp", "expert"), None),
        P(("dp", "expert"), None),
        P("expert", tensor, None),
        P("expert", None, tensor),
    )
    out_specs = (P(("dp", "expert"), tensor), P("expert", "dp", tensor))
    return jax.shard_map(
        per_device, mesh=fine, in_specs=in_specs, out_specs=out_specs, check_vma=False
    )
```

```python
import jax
import jax.numpy as jnp
from jax import lax
from jax.sharding import Mesh, PartitionSpec as P

BF = jnp.bfloat16
F32 = jnp.float32
XH, Z, CORE = 2, 8, 2
QUARTERS = XH * CORE
SWAP = [(0, 1), (1, 0)]


def exchange(pieces, axes):
    return lax.all_to_all(pieces, axes, split_axis=0, concat_axis=0, tiled=True)


def dot(a, b):
    return jnp.dot(a, b, preferred_element_type=F32)


def pick(index, pair):
    first = index == 0
    return jnp.where(first, pair[0], pair[1]), jnp.where(first, pair[1], pair[0])


def slots_of(routes, experts, capacity):
    flat = routes.reshape(-1)
    onehot = (flat[:, None] == jnp.arange(experts, dtype=jnp.int32)[None, :]).astype(jnp.int32)
    before = jnp.cumsum(onehot, axis=0) - onehot
    slot = jnp.sum(before * onehot, axis=1)
    target = flat * capacity + slot
    return jnp.arange(experts * capacity, dtype=jnp.int32)[:, None] == target[None, :]


def to_quarters(blocks, xh, core):
    near, sent = pick(xh, blocks)
    far = lax.ppermute(sent, "xh", SWAP)
    near_mine, near_sent = pick(core, near)
    far_mine, far_sent = pick(core, far)
    mine = jnp.stack([near_mine, far_mine])
    beside = lax.ppermute(jnp.stack([near_sent, far_sent]), "core", SWAP)
    return mine, beside


def per_device(tokens, cotangent, routes, route_weight, w_gate_up, w_down):
    tok_rows, width = tokens.shape
    experts = lax.axis_size("expert")
    dps = lax.axis_size("dp")
    top_count = routes.shape[1]
    capacity = min(tok_rows, 2 * tok_rows * top_count // experts)
    rows = experts * capacity
    hidden_units = w_gate_up.shape[2] // 2
    part = hidden_units // QUARTERS
    step = part // dps
    core = lax.axis_index("core")
    xh = lax.axis_index("xh")

    far_tokens = lax.ppermute(tokens, "xh", SWAP)

    matches = slots_of(routes, experts, capacity)
    select = jnp.sum(
        matches.reshape(rows, tok_rows, top_count).astype(F32), axis=2
    ).astype(BF)
    w = w_gate_up[0].reshape(width, 2, dps, CORE, XH, step).transpose(4, 3, 0, 1, 2, 5)
    w_mine, w_beside = to_quarters(
        w.reshape(XH, CORE, width, 2 * part), xh, core
    )

    weights_slot = jnp.sum(jnp.where(matches, route_weight.reshape(1, -1), 0.0), axis=1)
    sent = dot(select, jnp.concatenate([tokens, far_tokens, cotangent], axis=1))
    is_token = jnp.arange(3 * width, dtype=jnp.int32)[None, :] < 2 * width
    sent = (sent * jnp.where(is_token, 1.0, weights_slot[:, None])).astype(BF)
    mine = exchange(sent.reshape(experts, capacity, 3 * width), "expert")
    mine = mine.reshape(rows, 3 * width)
    beside = lax.ppermute(mine, "core", SWAP)

    partial = dot(mine[:, : 2 * width], w_mine.reshape(2 * width, 2 * part))
    partial += dot(beside[:, : 2 * width], w_beside.reshape(2 * width, 2 * part))
    moved = exchange(partial.astype(BF).reshape(Z, rows // Z, 2 * part), "z")
    gate_up = jnp.sum(moved.astype(F32), axis=0)
    hidden = (jax.nn.silu(gate_up[:, :part]) * gate_up[:, part:]).astype(BF)
    hidden = exchange(jnp.broadcast_to(hidden[None], (XH * Z,) + hidden.shape), ("xh", "z"))
    hidden = hidden.reshape(XH, rows, part)

    slot_grads = pick(core, jnp.stack([mine[:, 2 * width :], beside[:, 2 * width :]]))
    slot_grads = jnp.concatenate(slot_grads, axis=1)
    grads = []
    for columns in hidden:
        g = lax.dot_general(
            columns, slot_grads, (((0,), (0,)), ((), ())), preferred_element_type=F32
        ).astype(BF)
        g = [half.reshape(dps, step, width) for half in jnp.split(g, CORE, axis=1)]
        grads.append(jnp.stack(g, axis=1))
    grads = jnp.stack(grads, axis=2)
    moved = exchange(grads.reshape(dps * CORE, XH * step, width), ("dp", "core"))
    moved = moved.reshape(dps, QUARTERS * step, width)
    grad_share = jnp.sum(moved.astype(F32), axis=0)

    down = w_down[0].reshape(dps, CORE, XH, step, width).transpose(1, 2, 0, 3, 4)
    down_mine, down_sent = pick(core, down.reshape(CORE, XH, part, width))
    down_beside = lax.ppermute(down_sent, "core", SWAP)

    def terms(down):
        return dot(hidden[0], down[0]) + dot(hidden[1], down[1])

    outputs = terms(down_mine) + lax.ppermute(terms(down_beside), "core", SWAP)
    return outputs.astype(BF), grad_share[None]


def solution(mesh):
    dps, experts = mesh.shape["dp"], mesh.shape["expert"]
    fine = Mesh(
        mesh.devices.reshape(dps, experts, XH, Z, CORE), ("dp", "expert", "xh", "z", "core")
    )
    tensor = ("xh", "z", "core")
    in_specs = (
        P(("dp", "expert"), tensor),
        P(("dp", "expert"), tensor),
        P(("dp", "expert"), None),
        P(("dp", "expert"), None),
        P("expert", tensor, None),
        P("expert", None, tensor),
    )
    out_specs = (P(("dp", "expert"), tensor), P("expert", "dp", tensor))
    return jax.shard_map(
        per_device, mesh=fine, in_specs=in_specs, out_specs=out_specs, check_vma=False
    )
```

```python
import functools

import jax
import jax.numpy as jnp
from jax import lax
from jax.sharding import Mesh, PartitionSpec as P

BF = jnp.bfloat16
F32 = jnp.float32
XH, Z, CORE = 2, 8, 2
QUARTERS = XH * CORE
SWAP = [(0, 1), (1, 0)]


def exchange(pieces, axes):
    return lax.all_to_all(pieces, axes, split_axis=0, concat_axis=0, tiled=True)


def dot(a, b):
    return jnp.dot(a, b, preferred_element_type=F32)


def pick(index, pair):
    first = index == 0
    return jnp.where(first, pair[0], pair[1]), jnp.where(first, pair[1], pair[0])


def slots_of(routes, route_weight, experts, capacity):
    tokens = routes.shape[0]
    ids = jnp.arange(experts, dtype=jnp.int32)[:, None]
    named = [ids == column for column in routes.T[:, None, :]]
    gates = sum(jnp.where(n, w, 0.0) for n, w in zip(named, route_weight.T[:, None, :]))
    named = functools.reduce(jnp.logical_or, named)
    order = jnp.arange(tokens, dtype=jnp.int32)
    earlier = (order[:, None] < order[None, :]).astype(BF)
    slot = dot(named.astype(BF), earlier).astype(jnp.int32)
    slot = jnp.where(named, slot, -1)
    places = jnp.arange(capacity, dtype=jnp.int32)[None, :, None]
    match = slot[:, None, :] == places
    weights = jnp.sum(jnp.where(match, gates[:, None, :], 0.0), axis=2)
    return match.astype(BF).reshape(experts * capacity, tokens), weights.reshape(-1)


def to_quarters(blocks, xh, core):
    near, sent = pick(xh, blocks)
    far = lax.ppermute(sent, "xh", SWAP)
    near_mine, near_sent = pick(core, near)
    far_mine, far_sent = pick(core, far)
    mine = jnp.stack([near_mine, far_mine])
    beside = lax.ppermute(jnp.stack([near_sent, far_sent]), "core", SWAP)
    return mine, beside


def per_device(tokens, cotangent, routes, route_weight, w_gate_up, w_down):
    tok_rows, width = tokens.shape
    experts = lax.axis_size("expert")
    dps = lax.axis_size("dp")
    top_count = routes.shape[1]
    capacity = min(tok_rows, 2 * tok_rows * top_count // experts)
    rows = experts * capacity
    hidden_units = w_gate_up.shape[2] // 2
    part = hidden_units // QUARTERS
    step = part // dps
    core = lax.axis_index("core")
    xh = lax.axis_index("xh")

    far_tokens = lax.ppermute(tokens, "xh", SWAP)

    select, weights_slot = slots_of(routes, route_weight, experts, capacity)
    w = w_gate_up[0].reshape(width, 2, dps, CORE, XH, step).transpose(4, 3, 0, 1, 2, 5)
    w_mine, w_beside = to_quarters(
        w.reshape(XH, CORE, width, 2 * part), xh, core
    )

    sent = dot(select, jnp.concatenate([tokens, far_tokens, cotangent], axis=1))
    is_token = jnp.arange(3 * width, dtype=jnp.int32)[None, :] < 2 * width
    sent = (sent * jnp.where(is_token, 1.0, weights_slot[:, None])).astype(BF)
    mine = exchange(sent.reshape(experts, capacity, 3 * width), "expert")
    mine = mine.reshape(rows, 3 * width)
    beside = lax.ppermute(mine, "core", SWAP)

    partial = dot(mine[:, : 2 * width], w_mine.reshape(2 * width, 2 * part))
    partial += dot(beside[:, : 2 * width], w_beside.reshape(2 * width, 2 * part))
    moved = exchange(partial.astype(BF).reshape(Z, rows // Z, 2 * part), "z")
    gate_up = jnp.sum(moved.astype(F32), axis=0)
    hidden = (jax.nn.silu(gate_up[:, :part]) * gate_up[:, part:]).astype(BF)
    hidden = exchange(jnp.broadcast_to(hidden[None], (XH * Z,) + hidden.shape), ("xh", "z"))
    hidden = hidden.reshape(XH, rows, part)

    slot_grads = pick(core, jnp.stack([mine[:, 2 * width :], beside[:, 2 * width :]]))
    slot_grads = jnp.concatenate(slot_grads, axis=1)
    grads = []
    for columns in hidden:
        g = lax.dot_general(
            columns, slot_grads, (((0,), (0,)), ((), ())), preferred_element_type=F32
        ).astype(BF)
        g = [half.reshape(dps, step, width) for half in jnp.split(g, CORE, axis=1)]
        grads.append(jnp.stack(g, axis=1))
    grads = jnp.stack(grads, axis=2)
    moved = exchange(grads.reshape(dps * CORE, XH * step, width), ("dp", "core"))
    moved = moved.reshape(dps, QUARTERS * step, width)
    grad_share = jnp.sum(moved.astype(F32), axis=0)

    down = w_down[0].reshape(dps, CORE, XH, step, width).transpose(1, 2, 0, 3, 4)
    down_mine, down_sent = pick(core, down.reshape(CORE, XH, part, width))
    down_beside = lax.ppermute(down_sent, "core", SWAP)

    def terms(down):
        return dot(hidden[0], down[0]) + dot(hidden[1], down[1])

    outputs = terms(down_mine) + lax.ppermute(terms(down_beside), "core", SWAP)
    return outputs.astype(BF), grad_share[None]


def solution(mesh):
    dps, experts = mesh.shape["dp"], mesh.shape["expert"]
    fine = Mesh(
        mesh.devices.reshape(dps, experts, XH, Z, CORE), ("dp", "expert", "xh", "z", "core")
    )
    tensor = ("xh", "z", "core")
    in_specs = (
        P(("dp", "expert"), tensor),
        P(("dp", "expert"), tensor),
        P(("dp", "expert"), None),
        P(("dp", "expert"), None),
        P("expert", tensor, None),
        P("expert", None, tensor),
    )
    out_specs = (P(("dp", "expert"), tensor), P("expert", "dp", tensor))
    return jax.shard_map(
        per_device, mesh=fine, in_specs=in_specs, out_specs=out_specs, check_vma=False
    )
```
